256 devices in a mesh: row: 8 (over x, y_hi), col: 32 (over y_lo, z, core).
Axes of the slice: x: 4, y: 4 (y_hi: 2, y_lo: 2; y = y_hi * 2 + y_lo), z: 8, core: 2. Of those that a mesh axis runs over, the one named last changes fastest.
Arguments:
- features: bfloat16 [65536, 256], P(('row', 'col')), may hold values from -6 to 6
- weight: bfloat16 [256, 256], replicated, may hold values from -0.375 to 0.375
- cotangent: bfloat16 [65536, 256], P(('row', 'col')), may hold values from -6 to 6
- block_values: bfloat16 [8, 32, 32, 8, 128, 128], P('row', 'col'), may hold values from -0.046875 to 0.046875
- source_block: int32 [8, 32, 32, 8], P('row', 'col'), may hold values from 0 to 1
- target_block: int32 [8, 32, 32, 8], P('row', 'col'), may hold values from 0 to 15
- block_counts: int32 [8, 32, 32], P('row', 'col'), may hold values from 1 to 8, as said below
- block_order: int32 [256, 2], P(('row', 'col')), may hold values from 0 to 1, each once within a row
Outputs:
- activated: bfloat16 [65536, 256], P(('row', 'col'))
- input_grad: bfloat16 [65536, 256], P(('row', 'col'))
- weight_grad: bfloat16 [256, 256], replicated
The draws below stay inside these ranges and needn't reach their ends.
Inputs may be any that keep to these rules, and one draw needn't show every extreme that they name: `block_counts`: in every tile at least one source group has all 8 slots live; the others have from 1 up.
All inputs are finite; a program needn't handle non-finite values.
Results may differ from the reference program's by a relative error of at most 0.0067.
Values may be sent and summed in bfloat16 or wider, within the bound.
No kernel may reach another device: no remote copies, remote signals or barrier semaphores. Data moves between devices by JAX's collectives and lax.ppermute only.
A program may use at most 128 MiB of HBM per device.

```python
import jax
import jax.numpy as jnp
from jax import lax

F = 256
BS = 128
NBD = 2
MAXB = 8
GRID_R = 8
GRID_C = 32
DSTB = 16
SHARDS = 256
NODES = 65536


def draw_block_counts(key, part):
    key = jax.random.fold_in(key, 7)
    first_key, second_key, third_key = jax.random.split(key, 3)
    shape = (GRID_R, GRID_C, GRID_C)
    first_draw = jax.random.randint(first_key, shape, 0, MAXB)
    second_draw = jax.random.randint(second_key, shape, 0, MAXB)
    base_counts = 1 + jnp.maximum(first_draw, second_draw)
    picked = jax.random.randint(third_key, (GRID_R, GRID_C, 1), 0, GRID_C)
    full_group = jnp.arange(GRID_C)[None, None, :] == picked
    return jnp.where(full_group, MAXB, base_counts).astype(jnp.int32)


def touch_ends(entries, stream_key, least, high):
    shape = entries.shape
    index_at = [jax.random.randint(jax.random.fold_in(stream_key, axis), (), 0, shape[axis]) for axis in range(len(shape))]
    entries = entries.at[tuple(index_at)].set(least)
    longest = shape.index(max(shape))
    index_at[longest] = (index_at[longest] + 1) % shape[longest]
    return entries.at[tuple(index_at)].set(high)


def steps_of(rng, dims, cuts, smallest, top_value):
    factor_of = 1.0
    for axis_at, parts in cuts:
        draws = jax.random.uniform(jax.random.fold_in(jax.random.fold_in(rng, 6), axis_at), (parts,), jnp.float32, smallest / len(cuts), top_value / len(cuts))
        factor_of = factor_of * jnp.repeat(jnp.exp(draws), dims[axis_at] // parts).reshape((-1,) + (1,) * (len(dims) - 1 - axis_at))
    return factor_of


def centred(rng, extent, deviation, most, shards=(), held_as=jnp.bfloat16):
    result = jax.random.normal(rng, extent, jnp.float32) * deviation
    if len(shards) > 0:
        result = steps_of(rng, extent, shards, -0.22, 0.18) * result
    return jnp.clip(result, min=-most, max=most).astype(held_as)


def setup_inputs(seed: int = 0) -> dict:
    key_list = jax.random.split(jax.random.key(seed), 9)
    return {
        "features": centred(key_list[0], (NODES, F), 1.0, 6.0, ((0, 256),)),
        "weight": centred(key_list[1], (F, F), F ** -0.5, 0.375),
        "cotangent": centred(key_list[2], (NODES, F), 1.0, 6.0, ((0, 256),)),
        "block_values": centred(key_list[3], (GRID_R, GRID_C, GRID_C, MAXB, BS, BS), (BS * MAXB * GRID_C // NBD) ** -0.5, 0.046875, ((0, 8), (1, 32))),
        "source_block": touch_ends(jax.random.randint(key_list[4], (GRID_R, GRID_C, GRID_C, MAXB), 0, NBD), jax.random.fold_in(key_list[4], 1), 0, NBD - 1).astype(jnp.int32),
        "target_block": touch_ends(jax.random.randint(key_list[5], (GRID_R, GRID_C, GRID_C, MAXB), 0, DSTB), jax.random.fold_in(key_list[5], 1), 0, DSTB - 1).astype(jnp.int32),
        "block_counts": draw_block_counts(jax.random.fold_in(key_list[8], 71), 0),
        "block_order": jax.vmap(lambda own: jax.random.permutation(own, NBD))(jax.random.split(key_list[7], SHARDS)).reshape((SHARDS, NBD)).astype(jnp.int32),
    }


def silu_slope(preact):
    gate_sig = jax.nn.sigmoid(preact)
    return gate_sig * (1.0 + preact * (1.0 - gate_sig))

def reference(features, weight, cotangent, block_values, source_block, target_block, block_counts, block_order):
    shard_count = GRID_R * GRID_C
    feat_blocks = features.reshape(shard_count, NBD, BS, F).astype(jnp.float32)
    permuted = jnp.take_along_axis(feat_blocks, block_order.astype(jnp.int32)[:, :, None, None], axis=1)
    slot_ids = jnp.arange(MAXB, dtype=jnp.int32)
    live_mask = (slot_ids[None, None, None, :] < block_counts[..., None]).astype(jnp.float32)
    group_ids = jnp.arange(GRID_C, dtype=jnp.int32)

    def tile_parts(tile):
        row_idx = (tile // GRID_C).astype(jnp.int32)
        col_idx = (tile % GRID_C).astype(jnp.int32)
        tile_vals = block_values[row_idx, col_idx].astype(jnp.float32)
        src_idx = source_block[row_idx, col_idx]
        dst_idx = target_block[row_idx, col_idx]
        src_shard = (row_idx * GRID_C + group_ids)[:, None] + jnp.zeros_like(src_idx)
        dst_shard = dst_idx // NBD * GRID_C + col_idx
        dst_local = dst_idx % NBD
        return (tile_vals, src_idx, src_shard, dst_shard, dst_local, live_mask[row_idx, col_idx])

    def forward_tile(tile, totals):
        tile_vals, src_idx, src_shard, dst_shard, dst_local, mask_now = tile_parts(tile)
        picked = permuted[src_shard, src_idx]
        products = jnp.einsum('gkij,gkjf->gkif', tile_vals, picked) * mask_now[:, :, None, None]
        flat = (dst_shard * NBD + dst_local).reshape(-1).astype(jnp.int32)
        return totals.at[flat].add(products.reshape(-1, BS, F))
    zeros_acc = jnp.zeros((shard_count * NBD, BS, F), jnp.float32)
    totals = lax.fori_loop(0, shard_count, forward_tile, zeros_acc)
    aggregate = totals.reshape(NODES, F).astype(jnp.bfloat16)
    preact = jnp.dot(aggregate, weight, preferred_element_type=jnp.float32)
    activated = jax.nn.silu(preact).astype(jnp.bfloat16)
    delta = (cotangent.astype(jnp.float32) * silu_slope(preact)).astype(jnp.bfloat16)
    weight_grad = jnp.dot(aggregate.T, delta, preferred_element_type=jnp.float32) / jnp.sqrt(jnp.float32(NODES))
    back = jnp.dot(delta, weight.T, preferred_element_type=jnp.float32).astype(jnp.bfloat16)
    back_blocks = back.reshape(shard_count, NBD, BS, F).astype(jnp.float32)

    def backward_tile(tile, totals):
        tile_vals, src_idx, src_shard, dst_shard, dst_local, mask_now = tile_parts(tile)
        picked = back_blocks[dst_shard, dst_local]
        products = jnp.einsum('gkji,gkjf->gkif', tile_vals, picked) * mask_now[:, :, None, None]
        flat = (src_shard * NBD + src_idx).reshape(-1).astype(jnp.int32)
        return totals.at[flat].add(products.reshape(-1, BS, F))
    grad_perm = lax.fori_loop(0, shard_count, backward_tile, zeros_acc).reshape(shard_count, NBD, BS, F)
    inverse = jnp.argsort(block_order, axis=1).astype(jnp.int32)
    input_grad = jnp.take_along_axis(grad_perm, inverse[:, :, None, None], axis=1)
    return (activated, input_grad.reshape(NODES, F).astype(jnp.bfloat16), weight_grad.astype(jnp.bfloat16))
```

```python
import jax
import jax.numpy as jnp
from jax import lax
from jax.experimental import pallas as pl
from jax.experimental.pallas import tpu as pltpu
from jax.sharding import PartitionSpec as P

BS = 128
F = 256
ROWS = 8
COLS = 32
HALF = 16
SLOTS = 8
WROWS = F // ROWS
SEND = F + WROWS
ANY = pl.BlockSpec(memory_space=pl.ANY)
VM = pl.BlockSpec(memory_space=pltpu.VMEM)
SM = pl.BlockSpec(memory_space=pltpu.SMEM)


def params(mb):
    return pltpu.CompilerParams(vmem_limit_bytes=mb * 1024 * 1024)


def masked(code_ref, v_ref, j, g):
    rows = []
    for k in range(SLOTS):
        code = code_ref[g * SLOTS + k]
        value = v_ref[j, k]
        left = jnp.where(code == 0, 1.0, 0.0).astype(jnp.bfloat16)
        right = jnp.where(code == 1, 1.0, 0.0).astype(jnp.bfloat16)
        rows.append(jnp.concatenate([value * left, value * right], axis=1))
    return jnp.concatenate(rows, axis=0)


def value_copy(ids, v_hbm, vbuf, vsem, j):
    return pltpu.make_async_copy(v_hbm.at[ids[j]], vbuf.at[j], vsem.at[j])


def forward_kernel(ids, code, dst, xa, xb, v_hbm, out, vbuf, xbuf, acc, vsem, xsem):
    def x_copy(j):
        ref = xa if j < HALF else xb
        return pltpu.make_async_copy(ref.at[j % HALF], xbuf.at[j], xsem.at[j])

    for j in range(COLS):
        value_copy(ids, v_hbm, vbuf, vsem, j).start()
        x_copy(j).start()
    acc[...] = jnp.zeros_like(acc)

    def step(j, _):
        value_copy(ids, v_hbm, vbuf, vsem, j).wait()
        pltpu.make_async_copy(xa.at[0], xbuf.at[j], xsem.at[j]).wait()
        g = ids[j]
        products = jnp.dot(masked(code, vbuf, j, g), xbuf[j], preferred_element_type=jnp.float32)
        for k in range(SLOTS):
            t = dst[g * SLOTS + k]
            acc[t] = acc[t] + products[k * BS : (k + 1) * BS]
        return 0

    lax.fori_loop(0, COLS, step, 0)
    for t in range(2 * ROWS):
        out[t] = acc[t].astype(jnp.bfloat16)


def middle_kernel(recv, weight, cot, act, send):
    total = recv[0].astype(jnp.float32)
    for r in range(1, ROWS):
        total = total + recv[r].astype(jnp.float32)
    aggregate = total.astype(jnp.bfloat16)
    w = weight[...]
    preact = jnp.dot(aggregate, w, preferred_element_type=jnp.float32)
    gate = jax.nn.sigmoid(preact)
    act[...] = (preact * gate).astype(jnp.bfloat16)
    delta = (cot[...].astype(jnp.float32) * gate * (1.0 + preact * (1.0 - gate))).astype(jnp.bfloat16)
    back_t = lax.dot_general(w, delta, (((1,), (1,)), ((), ())), preferred_element_type=jnp.float32)
    back_t = back_t.astype(jnp.bfloat16)
    local = lax.dot_general(aggregate, delta, (((0,), (0,)), ((), ())), preferred_element_type=jnp.float32)
    local = local.astype(jnp.bfloat16)
    for r in range(ROWS):
        send[r, :F] = back_t
        send[r, F:] = local[r * WROWS : (r + 1) * WROWS]


def backward_kernel(ids, code, dst, recv, v_hbm, mine, other, wsum, vbuf, bbuf, obuf, vsem, osem):
    for j in range(COLS):
        value_copy(ids, v_hbm, vbuf, vsem, j).start()
    total = recv[0, F:].astype(jnp.float32)
    for r in range(1, ROWS):
        total = total + recv[r, F:].astype(jnp.float32)
    wsum[...] = total
    for r in range(ROWS):
        for b in range(2):
            bbuf[2 * r + b] = recv[r, :F, b * BS : (b + 1) * BS]

    def step(j, _):
        value_copy(ids, v_hbm, vbuf, vsem, j).wait()
        g = ids[j]
        cat = jnp.concatenate([bbuf[dst[g * SLOTS + k]] for k in range(SLOTS)], axis=1)
        out = jnp.dot(cat, masked(code, vbuf, j, g), preferred_element_type=jnp.float32)
        obuf[j] = out.astype(jnp.bfloat16)
        return 0

    def run(ref, first):
        def one(i, _):
            step(first + i, 0)
            pltpu.make_async_copy(obuf.at[first + i], ref.at[i], osem.at[first + i]).start()
            return 0

        lax.fori_loop(0, HALF, one, 0)

    run(other, HALF)
    run(mine, 0)
    for j in range(COLS):
        ref = mine if j < HALF else other
        pltpu.make_async_copy(obuf.at[j], ref.at[j % HALF], osem.at[j]).wait()


def end_kernel(order, a, b, out):
    total = (a[...].astype(jnp.float32) + b[...].astype(jnp.float32)).T
    for q in range(2):
        out[order[q]] = total[q * BS : (q + 1) * BS].astype(jnp.bfloat16)


def col_perm(move):
    pairs = []
    for yl in range(2):
        for z in range(8):
            for core in range(2):
                to_yl, to_z, to_core = move(yl, z, core)
                pairs.append((yl * 16 + z * 2 + core, to_yl * 16 + to_z % 8 * 2 + to_core))
    return pairs


UP = col_perm(lambda yl, z, core: (yl, z + 1, core))
DOWN = col_perm(lambda yl, z, core: (yl, z - 1, core))
SWAP_Y = col_perm(lambda yl, z, core: (1 - yl, z, core))
SWAP_C = col_perm(lambda yl, z, core: (yl, z, 1 - core))


def send(a, perm):
    return lax.ppermute(a, "col", perm)


def gather_col(own):
    chains = []
    for first in (own, send(own, SWAP_Y)):
        pieces = {0: first}
        up = down = first
        for s in range(1, 5):
            up = send(up, UP)
            pieces[8 - s] = up
            if s < 4:
                down = send(down, DOWN)
                pieces[s] = down
        chains += [pieces[i] for i in range(8)]
    mine = jnp.concatenate(chains, axis=0)
    return mine.reshape(HALF, F, F), send(mine, SWAP_C).reshape(HALF, F, F)


def scatter_col(mine, other):
    got = send(other, SWAP_C)

    def part(j):
        return mine[j].astype(jnp.float32) + got[j].astype(jnp.float32)

    ends = []
    for y in (1, 0):
        base = y * 8
        up = part(base + 4).astype(jnp.bfloat16)
        down = part(base + 5).astype(jnp.bfloat16)
        for s in (3, 2, 1):
            up = send(up, UP)
            up = (part(base + s) + up.astype(jnp.float32)).astype(jnp.bfloat16)
            down = send(down, DOWN)
            if s > 1:
                down = (part(base + 9 - s) + down.astype(jnp.float32)).astype(jnp.bfloat16)
        up = send(up, UP)
        ends.append(part(base) + up.astype(jnp.float32) + down.astype(jnp.float32))
    far, near = ends
    return near.astype(jnp.bfloat16), send(far.astype(jnp.bfloat16), SWAP_Y)


def sum_weight(total):
    for perm in (
        SWAP_C,
        SWAP_Y,
        col_perm(lambda yl, z, core: (yl, z ^ 1, core)),
        col_perm(lambda yl, z, core: (yl, z ^ 2, core)),
        col_perm(lambda yl, z, core: (yl, z ^ 4, core)),
    ):
        total = total + send(total, perm)
    rows = (total * (1.0 / 256.0)).astype(jnp.bfloat16)
    return lax.all_gather(rows, "row", axis=0, tiled=True)


def body(features, weight, cotangent, block_values, source_block, target_block, block_counts, block_order):
    me = lax.axis_index("col")
    place = jnp.arange(COLS, dtype=jnp.int32)
    yl = (me // 16) ^ (place // 8 % 2)
    z = (me // 2 + place) % 8
    core = (me % 2) ^ (place // 16)
    ids = (yl * 16 + z * 2 + core).astype(jnp.int32)
    live = jnp.arange(SLOTS, dtype=jnp.int32)[None, :] < block_counts[0, 0][:, None]
    code = jnp.where(live, source_block[0, 0], 2).reshape(-1)
    dst = target_block[0, 0].reshape(-1)
    values = block_values[0, 0]
    order = block_order[0]

    swapped = jnp.concatenate([features[BS:], features[:BS]], axis=0)
    ordered = jnp.where(order[0] == 0, features, swapped)
    xa, xb = gather_col(ordered)

    value_scratch = [pltpu.VMEM((COLS, SLOTS, BS, BS), jnp.bfloat16)]
    partial = pl.pallas_call(
        forward_kernel,
        out_shape=jax.ShapeDtypeStruct((2 * ROWS, BS, F), jnp.bfloat16),
        in_specs=[SM, SM, SM, ANY, ANY, ANY],
        out_specs=VM,
        scratch_shapes=value_scratch
        + [
            pltpu.VMEM((COLS, F, F), jnp.bfloat16),
            pltpu.VMEM((2 * ROWS, BS, F), jnp.float32),
            pltpu.SemaphoreType.DMA((COLS,)),
            pltpu.SemaphoreType.DMA((COLS,)),
        ],
        compiler_params=params(48),
        name="forward",
    )(ids, code, dst, xa, xb, values)
    received = lax.all_to_all(partial.reshape(ROWS * F, F), "row", 0, 0, tiled=True)

    activated, outgoing = pl.pallas_call(
        middle_kernel,
        out_shape=(
            jax.ShapeDtypeStruct((F, F), jnp.bfloat16),
            jax.ShapeDtypeStruct((ROWS, SEND, F), jnp.bfloat16),
        ),
        in_specs=[VM, VM, VM],
        out_specs=(VM, VM),
        compiler_params=params(32),
        name="middle",
    )(received.reshape(ROWS, F, F), weight, cotangent)
    backs = lax.all_to_all(outgoing.reshape(ROWS * SEND, F), "row", 0, 0, tiled=True)

    mine, other, wsum = pl.pallas_call(
        backward_kernel,
        out_shape=(
            jax.ShapeDtypeStruct((HALF, F, F), jnp.bfloat16),
            jax.ShapeDtypeStruct((HALF, F, F), jnp.bfloat16),
            jax.ShapeDtypeStruct((WROWS, F), jnp.float32),
        ),
        in_specs=[SM, SM, SM, VM, ANY],
        out_specs=(ANY, ANY, VM),
        scratch_shapes=value_scratch
        + [
            pltpu.VMEM((2 * ROWS, F, BS), jnp.bfloat16),
            pltpu.VMEM((COLS, F, F), jnp.bfloat16),
            pltpu.SemaphoreType.DMA((COLS,)),
            pltpu.SemaphoreType.DMA((COLS,)),
        ],
        compiler_params=params(48),
        name="backward",
    )(ids, code, dst, backs.reshape(ROWS, SEND, F), values)

    near, far = scatter_col(mine, other)
    weight_grad = sum_weight(wsum)
    input_grad = pl.pallas_call(
        end_kernel,
        out_shape=jax.ShapeDtypeStruct((2, BS, F), jnp.bfloat16),
        in_specs=[SM, VM, VM],
        out_specs=VM,
        compiler_params=params(32),
        name="end",
    )(order, near, far)
    return activated, input_grad.reshape(F, F), weight_grad


def solution(mesh):
    in_specs = (
        P(("row", "col"), None),
        P(),
        P(("row", "col"), None),
        P("row", "col", None, None, None, None),
        P("row", "col", None, None),
        P("row", "col", None, None),
        P("row", "col", None),
        P(("row", "col"), None),
    )
    out_specs = (P(("row", "col"), None), P(("row", "col"), None), P())
    return jax.shard_map(body, mesh=mesh, in_specs=in_specs, out_specs=out_specs, check_vma=False)
```

```python
import functools

import jax
import jax.numpy as jnp
from jax import lax
from jax.experimental import pallas as pl
from jax.experimental.pallas import tpu as pltpu
from jax.sharding import PartitionSpec as P

BS = 128
F = 256
ROWS = 8
COLS = 32
SLOTS = 8
WROWS = F // ROWS
SEND = 2 * F + 2 * WROWS
HBM = pl.BlockSpec(memory_space=pltpu.HBM)
VM = pl.BlockSpec(memory_space=pltpu.VMEM)
SM = pl.BlockSpec(memory_space=pltpu.SMEM)
DISTANCES = (0, 7, 1, 6, 2, 5, 3, 4)
HALF = 16
OWN = 0
SIBLING = 16


def params(mb):
    return pltpu.CompilerParams(vmem_limit_bytes=mb * 1024 * 1024)


def cost(flops, moved):
    return pl.CostEstimate(flops=flops, bytes_accessed=moved, transcendentals=0)


def products(groups):
    return cost(2 * groups * SLOTS * BS * BS * F, groups * 1024 * 1024)


def forward_groups(first, ids, src, dst, x, values, acc):
    for j in range(x.shape[0]):
        g = ids[first + j]
        for k in range(SLOTS):
            s = src[g * SLOTS + k]
            t = dst[g * SLOTS + k]
            picked = x[j, pl.ds(pl.multiple_of(s * BS, BS), BS)]
            acc[t] = acc[t] + jnp.dot(values[g, k], picked, preferred_element_type=jnp.float32)


def stream(first, ids, values, vbuf, vsem):
    groups = vbuf.shape[0]
    ends = [2, *range(6, groups, 4), groups]

    def copy(j):
        return pltpu.make_async_copy(values.at[ids[first + j]], vbuf.at[j], vsem.at[j])

    for j in range(groups):
        copy(j).start()

    def ready(j):
        for begin, end in zip([0] + ends, ends):
            if j == begin:
                for i in range(begin, end):
                    copy(i).wait()

    return ready


def forward_groups(first, ids, src, dst, x, values, acc, vbuf, vsem, begin):
    ready = stream(first, ids, values, vbuf, vsem)
    begin()
    for j in range(x.shape[0]):
        ready(j)
        g = ids[first + j]
        for k in range(SLOTS):
            s = src[g * SLOTS + k]
            t = dst[g * SLOTS + k]
            picked = x[j, pl.ds(pl.multiple_of(s * BS, BS), BS)]
            acc[t] = acc[t] + jnp.dot(vbuf[j, k], picked, preferred_element_type=jnp.float32)


def forward_first(first, ids, src, dst, x, values, acc, vbuf, vsem):
    def begin():
        acc[...] = jnp.zeros_like(acc)

    forward_groups(first, ids, src, dst, x, values, acc, vbuf, vsem, begin)


def forward_last(first, ids, src, dst, x, values, begun, out, vbuf, vsem, acc):
    def begin():
        acc[...] = begun[...]

    forward_groups(first, ids, src, dst, x, values, acc, vbuf, vsem, begin)
    for t in range(2 * ROWS):
        out[t] = acc[t].astype(jnp.bfloat16)


def middle_kernel(recv, weight, cot, act, send):
    total = recv[0].astype(jnp.float32)
    for r in range(1, ROWS):
        total = total + recv[r].astype(jnp.float32)
    aggregate = total.astype(jnp.bfloat16)
    w = weight[...]
    preact = jnp.dot(aggregate, w, preferred_element_type=jnp.float32)
    gate = jax.nn.sigmoid(preact)
    act[...] = (preact * gate).astype(jnp.bfloat16)
    delta = (cot[...].astype(jnp.float32) * gate * (1.0 + preact * (1.0 - gate))).astype(jnp.bfloat16)
    back_t = lax.dot_general(w, delta, (((1,), (1,)), ((), ())), preferred_element_type=jnp.float32)
    back_t = back_t.astype(jnp.bfloat16)
    local = lax.dot_general(aggregate, delta, (((0,), (0,)), ((), ())), preferred_element_type=jnp.float32)
    local = local.astype(jnp.bfloat16)
    for r in range(ROWS):
        for b in range(2):
            half = slice(b * BS, (b + 1) * BS)
            send[r, b * F : (b + 1) * F] = back_t[:, half]
            at = 2 * F + b * WROWS
            send[r, at : at + WROWS] = local[r * WROWS : (r + 1) * WROWS, half]


def backward_kernel(first, ids, code, dst, recv, values, out, vbuf, vsem, acc):
    ready = stream(first, ids, values, vbuf, vsem)
    for j in range(out.shape[0]):
        ready(j)
        g = ids[first + j]
        acc[j] = jnp.zeros((3, F, BS), jnp.float32)
        for k in range(SLOTS):
            c = code[g * SLOTS + k]
            t = dst[g * SLOTS + k]
            picked = recv[t // 2, pl.ds(pl.multiple_of(t % 2 * F, F), F)]
            acc[j, c] = acc[j, c] + jnp.dot(picked, vbuf[j, k], preferred_element_type=jnp.float32)
        for q in range(2):
            out[j, q * F : (q + 1) * F] = acc[j, q].astype(jnp.bfloat16)


def end_kernel(order, a, b, out):
    total = a[...].astype(jnp.float32) + b[...].astype(jnp.float32)
    for q in range(2):
        out[order[q]] = total[q * F : (q + 1) * F].T.astype(jnp.bfloat16)


def sum_kernel(z, *refs):
    out, scratch = refs[ROWS], refs[ROWS + 1]
    for i, distance in enumerate((0, 7, 6, 5, 4, 1, 2, 3)):
        scratch[(z[0] + distance) % 8] = refs[i][...]
    total = scratch[0].astype(jnp.float32)
    for i in range(1, 8):
        total = total + scratch[i].astype(jnp.float32)
    out[...] = (total * (1.0 / 256.0)).astype(jnp.bfloat16)


def weight_kernel(me, *refs):
    out = refs[-1]
    for k in range(ROWS):
        rows = pl.ds(pl.multiple_of((me[0] ^ k) * WROWS, WROWS), WROWS)
        out[rows, :BS] = refs[k][:WROWS]
        out[rows, BS:] = refs[k][WROWS:]


def col_perm(move):
    pairs = []
    for yl in range(2):
        for z in range(8):
            for core in range(2):
                to_yl, to_z, to_core = move(yl, z, core)
                pairs.append((yl * 16 + z * 2 + core, to_yl * 16 + to_z % 8 * 2 + to_core))
    return pairs


UP = col_perm(lambda yl, z, core: (yl, z + 1, core))
DOWN = col_perm(lambda yl, z, core: (yl, z - 1, core))
SWAP_Y = col_perm(lambda yl, z, core: (1 - yl, z, core))
SWAP_C = col_perm(lambda yl, z, core: (yl, z, 1 - core))
Z1, Z2, Z4 = [col_perm(lambda yl, z, core, bit=bit: (yl, z ^ bit, core)) for bit in (1, 2, 4)]


def send(a, perm):
    return lax.ppermute(a, "col", perm)


def across(a, k):
    return lax.ppermute(a, "row", [(r, r ^ k) for r in range(ROWS)])


def together(*arrays):
    return lax.optimization_barrier(arrays)


def call(kernel, out_shape, specs, name, mb, scratch=(), estimate=None):
    out_specs = jax.tree.map(lambda _: VM, out_shape)
    return pl.pallas_call(
        kernel,
        out_shape=out_shape,
        in_specs=specs,
        out_specs=out_specs,
        scratch_shapes=list(scratch),
        compiler_params=params(mb),
        cost_estimate=estimate,
        name=name,
    )


def bf(a):
    return a.astype(jnp.bfloat16)


def f32(a):
    return a.astype(jnp.float32)


def cat(*arrays):
    return jnp.concatenate(arrays, axis=0)


def buffers(groups):
    return [pltpu.VMEM((groups, SLOTS, BS, BS), jnp.bfloat16), pltpu.SemaphoreType.DMA((groups,))]


def forward(features, order, tables, values):
    swapped = cat(features[BS:], features[:BS])
    own = jnp.where(order[0] == 0, features, swapped)
    totals = jax.ShapeDtypeStruct((2 * ROWS + 1, BS, F), jnp.float32)

    def run(kernel, name, first, x, *begun, out=totals, scratch=()):
        x = x.reshape(-1, F, F)
        specs = [SM] * 3 + [VM, HBM] + [VM] * len(begun)
        scratch = buffers(x.shape[0]) + list(scratch)
        return call(
            functools.partial(kernel, first), out, specs, name, 48, scratch=scratch, estimate=products(x.shape[0])
        )(*tables, x, values, *begun)

    (own,) = together(own)
    pair = cat(own, send(own, SWAP_Y))
    ups, downs = [pair], [pair]
    for _ in range(3):
        ups.append(send(ups[-1], UP))
        downs.append(send(downs[-1], DOWN))
    last = send(ups[3][:F], UP), send(downs[3][F:], DOWN)
    near = cat(pair, ups[1], downs[1], ups[2], downs[2], ups[3], downs[3], *last)
    far = send(near, SWAP_C)
    begun = run(forward_first, "forward_1", OWN, near)
    out = jax.ShapeDtypeStruct((2 * ROWS, BS, F), jnp.bfloat16)
    scratch = [pltpu.VMEM(totals.shape, jnp.float32)]
    return run(forward_last, "forward_2", SIBLING, far, begun, out=out, scratch=scratch)


def backward(backs, tables, values, z):
    def run(name, first, groups=HALF):
        return call(
            functools.partial(backward_kernel, first),
            jax.ShapeDtypeStruct((groups, 2 * F, BS), jnp.bfloat16),
            [SM] * 3 + [VM, HBM],
            name,
            48,
            scratch=buffers(groups) + [pltpu.VMEM((groups, 3, F, BS), jnp.float32)],
            estimate=products(groups),
        )(*tables, backs, values)

    def hop(total, piece, perm):
        got = send(cat(bf(total), piece), perm)
        n = got.shape[0] - 2 * WROWS
        return f32(got[:n]), got[n:]

    def part(mine, got, lo, hi):
        return (f32(mine[lo:hi]) + f32(got[lo:hi])).reshape(-1, BS)

    w = jnp.sum(f32(backs[:, 2 * F :]), axis=0)
    other, got_w = together(run("backward_1", SIBLING), send(w, SWAP_Y))
    w = w + got_w
    got, got_w = together(send(other, SWAP_C), send(w, SWAP_C))
    mine = run("backward_2", OWN)
    w = bf(w + got_w)
    def pair(i):
        return part(mine, got, 2 * i, 2 * i + 2)

    up, up1 = hop(part(mine, got, 14, 15), w, UP)
    down, down1 = hop(part(mine, got, 15, 16), w, DOWN)
    zero = jnp.zeros_like(up)
    up, up2 = hop(pair(6) + cat(up, zero), up1, UP)
    down, down2 = hop(pair(5) + cat(zero, down), down1, DOWN)
    opposite = send(w, Z4)
    up, up3 = hop(pair(4) + up, up2, UP)
    down, down3 = hop(pair(3) + down, down2, DOWN)
    up = f32(send(bf(pair(2) + up), UP))
    down = f32(send(bf(pair(1) + down), DOWN))
    own = bf(pair(0) + up + down)
    far = send(own[2 * F :], SWAP_Y)
    piece = jax.ShapeDtypeStruct((2 * WROWS, BS), jnp.bfloat16)
    scratch = [pltpu.VMEM((8, 2 * WROWS, BS), jnp.bfloat16)]
    w = call(sum_kernel, piece, [SM] + [VM] * 8, "sum", 8, scratch=scratch)(
        z, w, up1, up2, up3, opposite, down1, down2, down3
    )
    pairs = cat(w, across(w, 1))
    rows = [pairs] + [across(pairs, k) for k in (2, 4, 6)]
    return own[: 2 * F], far, [half for a in rows for half in (a[: 2 * WROWS], a[2 * WROWS :])]


def body(features, weight, cotangent, block_values, source_block, target_block, block_counts, block_order):
    me = lax.axis_index("col").astype(jnp.int32)
    place = jnp.arange(COLS, dtype=jnp.int32)
    distance = jnp.repeat(jnp.array(DISTANCES * 2, jnp.int32), 2)
    ids = ((me // 16) ^ (place % 2)) * 16 + (me // 2 + distance) % 8 * 2 + ((me % 2) ^ (place // SIBLING))
    live = jnp.arange(SLOTS, dtype=jnp.int32)[None, :] < block_counts[0, 0][:, None]
    live = live.reshape(-1)
    src = source_block[0, 0].reshape(-1)
    dst = target_block[0, 0].reshape(-1)
    values = block_values[0, 0]
    order = block_order[0]
    bf16 = jnp.bfloat16

    partial = forward(features, order, (ids, src, jnp.where(live, dst, 2 * ROWS)), values)
    received = lax.all_to_all(partial.reshape(ROWS * F, F), "row", 0, 0, tiled=True)
    piece = jax.ShapeDtypeStruct((F, F), bf16)
    activated, outgoing = call(
        middle_kernel, (piece, jax.ShapeDtypeStruct((ROWS, SEND, BS), bf16)), [VM, VM, VM], "middle", 8
    )(received.reshape(ROWS, F, F), weight, cotangent)
    backs = lax.all_to_all(outgoing.reshape(ROWS * SEND, BS), "row", 0, 0, tiled=True)
    backs = backs.reshape(ROWS, SEND, BS)

    z = (me // 2 % 8).reshape(1)
    a, b, rows = backward(backs, (ids, jnp.where(live, src, 2), dst), values, z)
    row = lax.axis_index("row").astype(jnp.int32).reshape(1)
    weight_grad = call(weight_kernel, piece, [SM] + [VM] * ROWS, "weight", 8)(row, *rows)
    input_grad = call(end_kernel, jax.ShapeDtypeStruct((2, BS, F), bf16), [SM, VM, VM], "end", 8)(order, a, b)
    return activated, input_grad.reshape(F, F), weight_grad


def solution(mesh):
    in_specs = (
        P(("row", "col"), None),
        P(),
        P(("row", "col"), None),
        P("row", "col", None, None, None, None),
        P("row", "col", None, None),
        P("row", "col", None, None),
        P("row", "col", None),
        P(("row", "col"), None),
    )
    out_specs = (P(("row", "col"), None), P(("row", "col"), None), P())
    return jax.shard_map(body, mesh=mesh, in_specs=in_specs, out_specs=out_specs, check_vma=False)
```

```python
import functools

import jax
import jax.numpy as jnp
from jax import lax
from jax.experimental import pallas as pl
from jax.experimental.pallas import tpu as pltpu
from jax.sharding import PartitionSpec as P

BS = 128
F = 256
ROWS = 8
COLS = 32
SLOTS = 8
WROWS = 2 * F // ROWS
SEND = 2 * F + 2 * WROWS
HBM = pl.BlockSpec(memory_space=pltpu.HBM)
VM = pl.BlockSpec(memory_space=pltpu.VMEM)
SM = pl.BlockSpec(memory_space=pltpu.SMEM)
DISTANCES = (0, 7, 1, 6, 2, 5, 3, 4)
HALF = 16
OWN = 0
SIBLING = 16


def params(mb):
    return pltpu.CompilerParams(vmem_limit_bytes=mb * 1024 * 1024)


def cost(flops, moved):
    return pl.CostEstimate(flops=flops, bytes_accessed=moved, transcendentals=0)


def products(groups):
    return cost(2 * groups * SLOTS * BS * BS * F, groups * 1024 * 1024)


def forward_groups(first, ids, src, dst, x, values, acc):
    for j in range(x.shape[0]):
        g = ids[first + j]
        for k in range(SLOTS):
            s = src[g * SLOTS + k]
            t = dst[g * SLOTS + k]
            picked = x[j, pl.ds(pl.multiple_of(s * BS, BS), BS)]
            acc[t] = acc[t] + jnp.dot(values[g, k], picked, preferred_element_type=jnp.float32)


def order_kernel(order, features, out, sems):
    def copy(q):
        rows = pl.ds(pl.multiple_of(order[q] * BS, BS), BS)
        return pltpu.make_async_copy(features.at[rows], out.at[pl.ds(q * BS, BS)], sems.at[q])

    for q in range(2):
        copy(q).start()
    for q in range(2):
        copy(q).wait()


def stream(first, later, ids, values, vbuf, vsem, following, fsem):
    ends = [2, *range(6, HALF, 4), HALF]

    def copy(j):
        return pltpu.make_async_copy(values.at[ids[first + j]], vbuf.at[j], vsem.at[j])

    def ahead(j):
        return pltpu.make_async_copy(values.at[ids[later + j]], following.at[j], fsem.at[j])

    for j in range(HALF):
        copy(j).start()
    for j in range(HALF):
        ahead(j).start()

    def ready(j):
        for begin, end in zip([0] + ends, ends):
            if j == begin:
                for i in range(begin, end):
                    copy(i).wait()

    def finish():
        for j in range(HALF):
            ahead(j).wait()

    return ready, finish


def forward_group(g, block, src, dst, x, acc):
    for k in range(SLOTS):
        s = src[g * SLOTS + k]
        t = dst[g * SLOTS + k]
        picked = x[pl.ds(pl.multiple_of(s * BS, BS), BS)]
        acc[t] = acc[t] + jnp.dot(block[k], picked, preferred_element_type=jnp.float32)


def forward_first(ids, src, dst, x, values, acc, following, vbuf, vsem, fsem):
    ready, finish = stream(OWN, SIBLING, ids, values, vbuf, vsem, following, fsem)
    acc[...] = jnp.zeros_like(acc)
    for j in range(HALF):
        ready(j)
        forward_group(ids[OWN + j], vbuf.at[j], src, dst, x.at[j], acc)
    finish()


def forward_last(ids, src, dst, x, values, begun, *refs):
    acc = refs[5]
    acc[...] = begun[...]
    for j in range(HALF):
        forward_group(ids[SIBLING + j], values.at[j], src, dst, x.at[j], acc)
    for out, row in zip(refs[:5], (0, 2, 6, 4, 5)):
        for t in range(out.shape[0] // BS):
            out[t * BS : (t + 1) * BS] = acc[2 * row + t].astype(jnp.bfloat16)


def middle_kernel(own, got1, got3, other, weight, cot, act, send):
    total = own[:F].astype(jnp.float32) + other[...].astype(jnp.float32)
    total = total + got1[:F].astype(jnp.float32) + got3[:F].astype(jnp.float32)
    aggregate = total.astype(jnp.bfloat16)
    w = weight[...]
    preact = jnp.dot(aggregate, w, preferred_element_type=jnp.float32)
    gate = jax.nn.sigmoid(preact)
    act[...] = (preact * gate).astype(jnp.bfloat16)
    delta = (cot[...].astype(jnp.float32) * gate * (1.0 + preact * (1.0 - gate))).astype(jnp.bfloat16)
    back_t = lax.dot_general(w, delta, (((1,), (1,)), ((), ())), preferred_element_type=jnp.float32)
    back_t = back_t.astype(jnp.bfloat16)
    local = lax.dot_general(aggregate, delta, (((0,), (0,)), ((), ())), preferred_element_type=jnp.float32)
    local = local.astype(jnp.bfloat16)
    for r in range(ROWS):
        for b in range(2):
            half = slice(b * BS, (b + 1) * BS)
            send[r, b * F : (b + 1) * F] = back_t[:, half]
            at = 2 * F + b * WROWS
            send[r, at : at + WROWS] = local[r // 2 * WROWS : (r // 2 + 1) * WROWS, half]


def backward_group(g, block, code, dst, recv, out, acc):
    acc[...] = jnp.zeros((3, F, BS), jnp.float32)
    for k in range(SLOTS):
        c = code[g * SLOTS + k]
        t = dst[g * SLOTS + k]
        picked = recv[t // 2, pl.ds(pl.multiple_of(t % 2 * F, F), F)]
        acc[c] = acc[c] + jnp.dot(picked, block[k], preferred_element_type=jnp.float32)
    for q in range(2):
        out[q * F : (q + 1) * F] = acc[q].astype(jnp.bfloat16)


def backward_first(ids, code, dst, recv, values, out, following, vbuf, vsem, fsem, acc):
    ready, finish = stream(SIBLING, OWN, ids, values, vbuf, vsem, following, fsem)
    for j in range(HALF):
        ready(j)
        backward_group(ids[SIBLING + j], vbuf.at[j], code, dst, recv, out.at[j], acc.at[j])
    finish()


def backward_last(ids, code, dst, recv, values, out, acc):
    for j in range(HALF):
        backward_group(ids[OWN + j], values.at[j], code, dst, recv, out.at[j], acc.at[j])


def end_kernel(order, a, b, out):
    total = a[...].astype(jnp.float32) + b[...].astype(jnp.float32)
    for q in range(2):
        out[order[q]] = total[q * F : (q + 1) * F].T.astype(jnp.bfloat16)


def sum_kernel(z, *refs):
    out, scratch = refs[8], refs[9]
    for i, distance in enumerate((0, 7, 6, 5, 4, 1, 2, 3)):
        scratch[(z[0] + distance) % 8] = refs[i][...]
    total = scratch[0].astype(jnp.float32)
    for i in range(1, 8):
        total = total + scratch[i].astype(jnp.float32)
    out[...] = (total * (1.0 / 256.0)).astype(jnp.bfloat16)


def weight_kernel(me, *refs):
    out = refs[-1]
    for k in range(4):
        rows = pl.ds(pl.multiple_of((me[0] // 2 ^ k) * WROWS, WROWS), WROWS)
        out[rows, :BS] = refs[k][:WROWS]
        out[rows, BS:] = refs[k][WROWS:]


def col_perm(move):
    pairs = []
    for yl in range(2):
        for z in range(8):
            for core in range(2):
                to_yl, to_z, to_core = move(yl, z, core)
                pairs.append((yl * 16 + z * 2 + core, to_yl * 16 + to_z % 8 * 2 + to_core))
    return pairs


UP = col_perm(lambda yl, z, core: (yl, z + 1, core))
DOWN = col_perm(lambda yl, z, core: (yl, z - 1, core))
UP2 = col_perm(lambda yl, z, core: (yl, z + 2, core))
DOWN2 = col_perm(lambda yl, z, core: (yl, z - 2, core))
SWAP_Y = col_perm(lambda yl, z, core: (1 - yl, z, core))
SWAP_C = col_perm(lambda yl, z, core: (yl, z, 1 - core))


def send(a, perm):
    return lax.ppermute(a, "col", perm)


def across(a, k):
    return lax.ppermute(a, "row", [(r, r ^ k) for r in range(ROWS)])


def together(*arrays):
    return lax.optimization_barrier(arrays)


def call(kernel, out_shape, specs, name, mb, scratch=(), estimate=None):
    out_specs = jax.tree.map(lambda _: VM, out_shape)
    return pl.pallas_call(
        kernel,
        out_shape=out_shape,
        in_specs=specs,
        out_specs=out_specs,
        scratch_shapes=list(scratch),
        compiler_params=params(mb),
        cost_estimate=estimate,
        name=name,
    )


def bf(a):
    return a.astype(jnp.bfloat16)


def f32(a):
    return a.astype(jnp.float32)


def cat(*arrays):
    return jnp.concatenate(arrays, axis=0)


BLOCKS = (HALF, SLOTS, BS, BS)
STREAM = [pltpu.VMEM(BLOCKS, jnp.bfloat16)] + [pltpu.SemaphoreType.DMA((HALF,))] * 2


def forward(features, order, tables, values):
    scratch = [pltpu.SemaphoreType.DMA((2,))]
    own = call(
        order_kernel, jax.ShapeDtypeStruct((F, F), jnp.bfloat16), [SM, HBM], "order", 60, scratch=scratch
    )(order, features)
    totals = jax.ShapeDtypeStruct((2 * ROWS + 1, BS, F), jnp.float32)

    pieces = {}
    for y, first in enumerate((own, send(own, SWAP_Y))):
        pieces[0, y] = up = down = first
        for distance in range(1, 4):
            pieces[8 - distance, y] = up = send(up, UP)
            pieces[distance, y] = down = send(down, DOWN)
    pieces[4, 0] = send(pieces[5, 0], UP)
    pieces[4, 1] = send(pieces[2, 1], DOWN2)
    near = cat(*(pieces[distance, y] for distance in DISTANCES for y in range(2)))
    far = send(near, SWAP_C)
    blocks = jax.ShapeDtypeStruct(BLOCKS, jnp.bfloat16)
    begun, blocks = call(
        forward_first, (totals, blocks), [SM] * 3 + [VM, HBM], "forward_1", 44, STREAM, products(HALF)
    )(*tables, near.reshape(HALF, F, F), values)
    out = tuple(jax.ShapeDtypeStruct((n * F, F), jnp.bfloat16) for n in (2, 2, 2, 1, 1))
    scratch = [pltpu.VMEM(totals.shape, jnp.float32)]
    own, near1, near3, far0, far1 = call(
        forward_last, out, [SM] * 3 + [VM] * 3, "forward_2", 40, scratch, products(HALF)
    )(*tables, far.reshape(HALF, F, F), blocks, begun)
    far0, far1 = across(far0, 2), across(far1, 6)
    near3 = cat(bf(f32(near3[:F]) + f32(far0)), near3[F:])
    near1 = cat(near1[:F], bf(f32(near1[F:]) + f32(far1)))
    got1, got3 = across(near1, 2), across(near3, 6)
    other = across(bf(f32(own[F:]) + f32(got1[F:]) + f32(got3[F:])), 1)
    return own, got1, got3, other


def backward(backs, tables, values, z):
    def hop(total, piece, perm):
        got = send(cat(bf(total), piece), perm)
        n = got.shape[0] - 2 * WROWS
        return f32(got[:n]), got[n:]

    def part(mine, got, lo, hi):
        return (f32(mine[lo:hi]) + f32(got[lo:hi])).reshape(-1, BS)

    sums = jax.ShapeDtypeStruct((HALF, 2 * F, BS), jnp.bfloat16)
    acc = [pltpu.VMEM((HALF, 3, F, BS), jnp.float32)]
    blocks = jax.ShapeDtypeStruct(BLOCKS, jnp.bfloat16)
    other, blocks = call(
        backward_first, (sums, blocks), [SM] * 3 + [VM, HBM], "backward_1", 44, STREAM + acc, products(HALF)
    )(*tables, backs, values)
    w = jnp.sum(f32(backs[:, 2 * F :]), axis=0)
    other, got_w = together(other, send(w, SWAP_Y))
    w = w + got_w
    got, got_w = together(send(other, SWAP_C), send(w, SWAP_C))
    mine = call(backward_last, sums, [SM] * 3 + [VM] * 2, "backward_2", 40, acc, products(HALF))(
        *tables, backs, blocks
    )
    w = bf(w + got_w)
    def pair(i):
        return part(mine, got, 2 * i, 2 * i + 2)

    zero = jnp.zeros((2 * F, BS), jnp.float32)
    up, up1 = hop(pair(6), w, UP)
    down, down1 = hop(pair(5), w, DOWN)
    near, up2 = hop(part(mine, got, 14, 15), w, UP2)
    far, down2 = hop(part(mine, got, 15, 16), w, DOWN2)
    up, up3 = hop(pair(4) + up + cat(near, zero), up2, UP)
    down, down3 = hop(pair(3) + down + cat(zero, far), down2, DOWN)
    up, up4 = hop(pair(2) + up, up3, UP)
    down = f32(send(bf(pair(1) + down), DOWN))
    own = bf(pair(0) + up + down)
    far = send(own[2 * F :], SWAP_Y)
    piece = jax.ShapeDtypeStruct((2 * WROWS, BS), jnp.bfloat16)
    scratch = [pltpu.VMEM((8, 2 * WROWS, BS), jnp.bfloat16)]
    w = call(sum_kernel, piece, [SM] + [VM] * 8, "sum", 8, scratch=scratch)(
        z, w, up1, up2, up3, up4, down1, down2, down3
    )
    return own[: 2 * F], far, [w] + [across(w, k) for k in (2, 4, 6)]


def body(features, weight, cotangent, block_values, source_block, target_block, block_counts, block_order):
    me = lax.axis_index("col").astype(jnp.int32)
    place = jnp.arange(COLS, dtype=jnp.int32)
    distance = jnp.repeat(jnp.array(DISTANCES * 2, jnp.int32), 2)
    ids = ((me // 16) ^ (place % 2)) * 16 + (me // 2 + distance) % 8 * 2 + ((me % 2) ^ (place // SIBLING))
    live = jnp.arange(SLOTS, dtype=jnp.int32)[None, :] < block_counts[0, 0][:, None]
    live = live.reshape(-1)
    src = source_block[0, 0].reshape(-1)
    dst = target_block[0, 0].reshape(-1)
    values = block_values[0, 0]
    order = block_order[0]
    bf16 = jnp.bfloat16

    row = lax.axis_index("row").astype(jnp.int32)
    sums = forward(features, order, (ids, src, jnp.where(live, dst ^ (2 * row), 2 * ROWS)), values)
    piece = jax.ShapeDtypeStruct((F, F), bf16)
    activated, outgoing = call(
        middle_kernel, (piece, jax.ShapeDtypeStruct((ROWS, SEND, BS), bf16)), [VM] * 6, "middle", 8
    )(*sums, weight, cotangent)
    backs = lax.all_to_all(outgoing.reshape(ROWS * SEND, BS), "row", 0, 0, tiled=True)
    backs = backs.reshape(ROWS, SEND, BS)

    z = (me // 2 % 8).reshape(1)
    a, b, rows = backward(backs, (ids, jnp.where(live, src, 2), dst), values, z)
    weight_grad = call(weight_kernel, piece, [SM] + [VM] * 4, "weight", 8)(row.reshape(1), *rows)
    input_grad = call(end_kernel, jax.ShapeDtypeStruct((2, BS, F), bf16), [SM, VM, VM], "end", 8)(order, a, b)
    return activated, input_grad.reshape(F, F), weight_grad


def solution(mesh):
    in_specs = (
        P(("row", "col"), None),
        P(),
        P(("row", "col"), None),
        P("row", "col", None, None, None, None),
        P("row", "col", None, None),
        P("row", "col", None, None),
        P("row", "col", None),
        P(("row", "col"), None),
    )
    out_specs = (P(("row", "col"), None), P(("row", "col"), None), P())
    return jax.shard_map(body, mesh=mesh, in_specs=in_specs, out_specs=out_specs, check_vma=False)
```
